32 devices in a mesh: box: 8 (over z, core), sub: 4 (over y, x).
Axes of the slice: x: 2, y: 2, z: 4, core: 2. Of those that a mesh axis runs over, the one named last changes fastest.
Arguments:
- right_side: float32 [64, 128, 256], P('box', 'sub'), may hold values from -6 to 6
- beta: float32 [64, 128, 256], P('box', 'sub'), may hold values from 0.2 to 5
Outputs:
- pressure: float32 [64, 128, 256], P('box', 'sub')
- residual: float32 [64, 128, 256], P('box', 'sub')
The draws below stay inside these ranges and needn't reach their ends.
All inputs are finite; a program needn't handle non-finite values.
Results may differ from the reference program's by a relative error of at most 0.0003.
Values sent between devices are 32-bit elements; how exact they have to be, the bound alone decides.
A program may use at most 192 MiB of HBM per device.

```python
import math
import jax
import jax.numpy as jnp
from jax import lax

ITERS = 8
NX = 64
NY = 128
NZ = 256


def draw_right_side(key, part):
    key = jax.random.fold_in(key, 11)
    values = jax.random.normal(key, (NX, NY, NZ), jnp.float32)
    return jnp.clip(values, -6.0, 6.0)


def block_levels(own_key, dims, shards, smallest, largest):
    factor_of, own = 1.0, jax.random.fold_in(own_key, 6)
    for dim, blocks in shards:
        draws = jnp.exp(jax.random.uniform(jax.random.fold_in(own, dim), (blocks,), jnp.float32, smallest / len(shards), largest / len(shards)))
        factor_of = factor_of * jnp.repeat(draws, dims[dim] // blocks).reshape([-1 if axis == dim else 1 for axis in range(len(dims))])
    return factor_of


def setup_inputs(seed: int = 0) -> dict:
    arg_keys = jax.random.split(jax.random.key(seed), 3)
    right_side = draw_right_side(jax.random.fold_in(arg_keys[2], 71), 0)
    beta = jnp.clip(jnp.exp(math.log(5.0) - 3.218876 * jax.random.uniform(arg_keys[1], (NX, NY, NZ), jnp.float32) ** block_levels(arg_keys[1], (NX, NY, NZ), ((0, 8), (1, 4)), -0.2, 0.2)), 0.2, 5.0)
    return dict(right_side=right_side, beta=beta)


def sides(padded):
    return (padded[:-2, 1:-1, 1:-1], padded[2:, 1:-1, 1:-1], padded[1:-1, :-2, 1:-1],
            padded[1:-1, 2:, 1:-1], padded[1:-1, 1:-1, :-2], padded[1:-1, 1:-1, 2:])


def coefficients(beta_pad):
    center = beta_pad[1:-1, 1:-1, 1:-1]
    faces = jnp.stack([0.5 * (center + side) for side in sides(beta_pad)])
    return faces, jnp.sum(faces, axis=0)


def neighbour_sum(padded, faces):
    total = jnp.zeros(faces.shape[1:], faces.dtype)
    for index, side in enumerate(sides(padded)):
        total = total + faces[index] * side
    return total


def pad_whole(field):
    return jnp.pad(field, 1)


def red_cells(shape):
    parity = (lax.broadcasted_iota(jnp.int32, shape, 0) + lax.broadcasted_iota(jnp.int32, shape, 1)
              + lax.broadcasted_iota(jnp.int32, shape, 2)) % 2
    return parity == 0


def relax(field, source, faces, diag, mask):
    return jnp.where(mask, (source + neighbour_sum(pad_whole(field), faces)) / diag, field)


def sweep(field, source, faces, diag):
    red = red_cells(field.shape)
    field = relax(field, source, faces, diag, red)
    return relax(field, source, faces, diag, jnp.logical_not(red))


def remainder(field, source, faces, diag):
    return source - (diag * field - neighbour_sum(pad_whole(field), faces))


def restrict(field, factor):
    nx, ny, nz = field.shape
    return field.reshape(nx // 2, 2, ny // 2, 2, nz // 2, 2).sum(axis=(1, 3, 5)) * factor


def prolong(field):
    return jnp.repeat(jnp.repeat(jnp.repeat(field, 2, 0), 2, 1), 2, 2)


def reference(right_side, beta):
    faces_f, diag_f = coefficients(pad_whole(beta))
    pressure_pre = sweep(jnp.zeros_like(right_side), right_side, faces_f, diag_f)
    fine_resid = remainder(pressure_pre, right_side, faces_f, diag_f)
    medium_beta = restrict(beta, 0.125)
    medium_rhs = restrict(fine_resid, 0.5)
    faces_m, diag_m = coefficients(pad_whole(medium_beta))
    medium_pre = sweep(jnp.zeros_like(medium_rhs), medium_rhs, faces_m, diag_m)
    medium_resid = remainder(medium_pre, medium_rhs, faces_m, diag_m)
    coarse_beta = restrict(medium_beta, 0.125)
    coarse_rhs = restrict(medium_resid, 0.5)
    faces_c, diag_c = coefficients(pad_whole(coarse_beta))
    solved = jnp.zeros_like(coarse_rhs)
    resid = coarse_rhs
    precond = resid / diag_c
    direction = precond
    rz_now = jnp.sum(resid * precond)
    for step in range(ITERS):
        image = diag_c * direction - neighbour_sum(pad_whole(direction), faces_c)
        alpha = rz_now / jnp.sum(direction * image)
        solved = solved + alpha * direction
        resid = resid - alpha * image
        precond = resid / diag_c
        rz_next = jnp.sum(resid * precond)
        direction = precond + (rz_next / rz_now) * direction
        rz_now = rz_next
    medium_post = sweep(medium_pre + prolong(solved), medium_rhs, faces_m, diag_m)
    pressure = sweep(pressure_pre + prolong(medium_post), right_side, faces_f, diag_f)
    residual = remainder(pressure, right_side, faces_f, diag_f)
    return pressure, residual
```

```python
import functools

import jax
import jax.numpy as jnp
from jax import lax
from jax.experimental import pallas as pl
from jax.experimental.pallas import tpu as pltpu
from jax.sharding import PartitionSpec as P

ITERS = 8
HB = 5
HG = 4
HY = 8
HM = 4
DIRECTIONS = [(dx, dy) for dx in (-1, 0, 1) for dy in (-1, 0, 1) if (dx, dy) != (0, 0)]
HIGHEST = lax.Precision.HIGHEST


def span(step, size, width, halo):
    if step == 0:
        return 0, halo, size
    if step > 0:
        return size - width, halo - width, width
    return 0, halo + size, width


def shifted(value, step, axis):
    return pltpu.roll(value, (-step) % value.shape[axis], axis)


def kernel(nb, ns, g_in, b_in, p_out, r_out, B, G, CX, CYP, CYM, CZP, CZM, D, I, V, TMP,
           BM, GM, MX, MYP, MYM, MZP, MZM, DM, IM, W, PM, CB, CR, XC, CXP, CXM, KYP, KYM, KZP, KZM, DC, IC,
           RR, PP, own_sem, fine_send, fine_recv, med_send, med_recv, box_send, box_recv, sub_send, sub_recv):
    nx, ny, nz = g_in.shape
    mx, my, mz = nx // 2, ny // 2, nz // 2
    cy = my // 2
    rows, mrows = ny + 2 * HY, my + 2 * HY
    box, sub = lax.axis_index("box"), lax.axis_index("sub")

    def exists(dx, dy):
        ok = None
        for step, at, size in ((dx, box, nb), (dy, sub, ns)):
            here = None if step == 0 else (at + step < size if step > 0 else at + step >= 0)
            ok = here if ok is None else (ok if here is None else jnp.logical_and(ok, here))
        return ok

    def halo(src, dst, own, width_x, halo_x, sends, recvs, from_ext):
        out = []
        for k, (dx, dy) in enumerate(DIRECTIONS):
            sx, tx, lx = span(dx, own[0], width_x, halo_x)
            sy, ty, ly = span(dy, own[1], HY, HY)
            if from_ext:
                sx, sy = sx + halo_x, sy + HY
            out.append(pltpu.make_async_remote_copy(
                src_ref=src.at[pl.ds(sx, lx), pl.ds(sy, ly), :],
                dst_ref=dst.at[pl.ds(tx, lx), pl.ds(ty, ly), :],
                send_sem=sends.at[k], recv_sem=recvs.at[k],
                device_id={"box": box + dx, "sub": sub + dy},
                device_id_type=pl.DeviceIdType.MESH))
        return out

    def start(copies):
        for (dx, dy), copy in zip(DIRECTIONS, copies):
            pl.when(exists(dx, dy))(copy.start)

    def wait_recv(copies):
        for (dx, dy), copy in zip(DIRECTIONS, copies):
            pl.when(exists(-dx, -dy))(copy.wait_recv)

    def wait_send(copies):
        for (dx, dy), copy in zip(DIRECTIONS, copies):
            pl.when(exists(dx, dy))(copy.wait_send)

    def clear(dst, own, width_x, halo_x):
        for dx, dy in DIRECTIONS:
            _, tx, lx = span(dx, own[0], width_x, halo_x)
            _, ty, ly = span(dy, own[1], HY, HY)

            @pl.when(jnp.logical_not(exists(-dx, -dy)))
            def _():
                dst[pl.ds(tx, lx), pl.ds(ty, ly), :] = jnp.zeros((lx, ly, dst.shape[2]), jnp.float32)

    beta_halo = halo(b_in, B, (nx, ny), HB, HB, fine_send.at[0], fine_recv.at[0], False)
    rhs_halo = halo(g_in, G, (nx, ny), HG, HB, fine_send.at[1], fine_recv.at[1], False)
    own_b = pltpu.make_async_copy(b_in, B.at[pl.ds(HB, nx), pl.ds(HY, ny), :], own_sem.at[0])
    own_g = pltpu.make_async_copy(g_in, G.at[pl.ds(HB, nx), pl.ds(HY, ny), :], own_sem.at[1])
    own_b.start()
    start(beta_halo)
    start(rhs_halo)
    own_g.start()

    pair_sum = (lax.broadcasted_iota(jnp.int32, (nz, mz), 0) >> 1
                == lax.broadcasted_iota(jnp.int32, (nz, mz), 1)).astype(jnp.float32)
    spread = (lax.broadcasted_iota(jnp.int32, (mz, nz), 1) >> 1
              == lax.broadcasted_iota(jnp.int32, (mz, nz), 0)).astype(jnp.float32)

    def restrict(planes, factor):
        n = planes.shape[0]
        TMP[0:n, :] = jnp.dot(planes, pair_sum, precision=HIGHEST, preferred_element_type=jnp.float32)
        return (TMP[pl.ds(0, n // 2, stride=2), :] + TMP[pl.ds(1, n // 2, stride=2), :]) * factor

    def pack(planes):
        return jnp.concatenate([planes[0] + planes[1], planes[2] + planes[3]], axis=1)

    def gather(buffer, index):
        def block(b, s, size):
            return buffer.at[pl.ds(b, size), pl.ds(pl.multiple_of(s * cy, cy), cy), :]
        first = [pltpu.make_async_remote_copy(
            src_ref=block(box, sub, 1), dst_ref=block(box, sub, 1),
            send_sem=box_send.at[index, k], recv_sem=box_recv.at[index, k],
            device_id={"box": lax.rem(box + k + 1, nb), "sub": sub}, device_id_type=pl.DeviceIdType.MESH)
            for k in range(nb - 1)]
        second = [pltpu.make_async_remote_copy(
            src_ref=block(0, sub, nb), dst_ref=block(0, sub, nb),
            send_sem=sub_send.at[index, k], recv_sem=sub_recv.at[index, k],
            device_id={"box": box, "sub": lax.rem(sub + k + 1, ns)}, device_id_type=pl.DeviceIdType.MESH)
            for k in range(ns - 1)]
        return first, second

    own_b.wait()
    for k in range(mx):
        summed = B[HB + 2 * k, pl.ds(HY, ny), :] + B[HB + 2 * k + 1, pl.ds(HY, ny), :]
        BM[HM + k, pl.ds(HY, my), :] = restrict(summed, 0.125)
    bm_halo = halo(BM, BM, (mx, my), HM, HM, med_send.at[0], med_recv.at[0], True)
    start(bm_halo)
    own_rows = pl.ds(pl.multiple_of(sub * cy, cy), cy)
    CB[box, own_rows, :] = restrict(pack([BM[HM + k, pl.ds(HY, my), :] for k in range(mx)]), 0.125)
    cb_first, cb_second = gather(CB, 0)
    for copy in cb_first:
        copy.start()
    clear(B, (nx, ny), HB, HB)
    clear(G, (nx, ny), HG, HB)
    clear(BM, (mx, my), HM, HM)
    clear(GM, (mx, my), HM, HM)
    clear(PM, (mx, my), HM, HM)

    def parity(shape):
        return (lax.broadcasted_iota(jnp.int32, shape, 0) + lax.broadcasted_iota(jnp.int32, shape, 1)) & 1

    def setup_plane(e, b_ref, x_ref, yp, ym, zp, zm, d_ref, i_ref):
        b = b_ref[e]
        lane = lax.broadcasted_iota(jnp.int32, b.shape, 1)
        half = 0.5 * b
        up, down = shifted(half, 1, 0), shifted(half, -1, 0)
        right = jnp.where(lane == b.shape[1] - 1, 0.0, shifted(half, 1, 1))
        left = jnp.where(lane == 0, 0.0, shifted(half, -1, 1))
        before, after = 0.5 * b_ref[e - 1], 0.5 * b_ref[e + 1]
        x_ref[e] = half + after
        yp[e] = half + up
        ym[e] = half + down
        zp[e] = jnp.where(lane == b.shape[1] - 1, 0.0, half + right)
        zm[e] = jnp.where(lane == 0, 0.0, half + left)
        diag = 6.0 * half + ((before + after) + (up + down) + (right + left))
        inverse = jnp.where(b > 0.0, 1.0 / diag, 0.0)
        d_ref[e] = diag
        i_ref[e] = inverse
        return inverse

    def neighbours(e, v_ref, x_ref, yp, ym, zp, zm, cut=slice(None)):
        v = v_ref[e]
        total = x_ref[e] * v_ref[e + 1] + x_ref[e - 1] * v_ref[e - 1]
        total += yp[e] * shifted(v, 1, 0) + ym[e] * shifted(v, -1, 0)
        total += zp[e] * shifted(v, 1, 1) + zm[e] * shifted(v, -1, 1)
        return total, v

    fine = (CX, CYP, CYM, CZP, CZM)
    medium = (MX, MYP, MYM, MZP, MZM)
    fine_parity, medium_parity = parity((rows, nz)), parity((mrows, mz))

    def fine_relax(colour, low, high):
        @pl.loop(low, high)
        def _(e):
            total, v = neighbours(e, V, *fine)
            V[e] = jnp.where(fine_parity == ((e + HB + colour) & 1), (G[e] + total) * I[e], v)

    def medium_relax(colour, low, high):
        @pl.loop(low, high)
        def _(e):
            total, v = neighbours(e, W, *medium)
            W[e] = jnp.where(medium_parity == ((e + HM + colour) & 1), (GM[e] + total) * IM[e], v)

    own_g.wait()
    wait_recv(beta_halo)
    wait_recv(rhs_halo)

    V[0] = jnp.zeros((rows, nz), jnp.float32)
    V[nx + 2 * HB - 1] = jnp.zeros((rows, nz), jnp.float32)

    @pl.loop(1, nx + 2 * HB - 1)
    def _(e):
        inverse = setup_plane(e, B, *fine, D, I)
        V[e] = jnp.where(fine_parity == ((e + HB) & 1), G[e] * inverse, 0.0)

    fine_relax(1, 2, nx + 2 * HB - 2)

    def fine_residual(e):
        total, v = neighbours(e, V, *fine)
        return (G[e] - (D[e] * v - total))[HY:HY + ny]

    @pl.loop(0, mx)
    def _(k):
        summed = fine_residual(HB + 2 * k) + fine_residual(HB + 2 * k + 1)
        GM[HM + k, pl.ds(HY, my), :] = restrict(summed, 0.5)

    gm_halo = halo(GM, GM, (mx, my), HM, HM, med_send.at[1], med_recv.at[1], True)
    start(gm_halo)

    wait_recv(bm_halo)
    MX[0] = 0.5 * (BM[0] + BM[1])

    @pl.loop(1, mx + 2 * HM - 1)
    def _(e):
        setup_plane(e, BM, *medium, DM, IM)

    for copy in cb_first:
        copy.wait_recv()
    for copy in cb_second:
        copy.start()
    wait_recv(gm_halo)

    @pl.loop(HM - 2, HM + mx + 2)
    def _(e):
        W[e] = jnp.where(medium_parity == ((e + HM) & 1), GM[e] * IM[e], 0.0)

    medium_relax(1, HM - 1, HM + mx + 1)
    residuals = []
    for k in range(mx):
        total, v = neighbours(HM + k, W, *medium)
        residuals.append((GM[HM + k] - (DM[HM + k] * v - total))[HY:HY + my])
        PM[HM + k, pl.ds(HY, my), :] = v[HY:HY + my]
    CR[box, own_rows, :] = restrict(pack(residuals), 0.5)
    cr_first, cr_second = gather(CR, 1)
    for copy in cr_first:
        copy.start()
    pm_halo = halo(PM, PM, (mx, my), HM, HM, med_send.at[2], med_recv.at[2], True)
    start(pm_halo)

    for copy in cb_second:
        copy.wait_recv()
    crows = ns * cy
    cz = mz // 2
    lane = lax.broadcasted_iota(jnp.int32, (crows, mz), 1)
    row = lax.broadcasted_iota(jnp.int32, (crows, mz), 0)
    low = lane < cz
    z = lane & (cz - 1)
    zero = jnp.zeros((crows, mz), jnp.float32)
    for k in range(nb):
        half = 0.5 * CB[k]
        swap = shifted(half, cz, 1)
        swap_before = 0.5 * shifted(CB[k - 1], cz, 1) if k > 0 else zero
        swap_after = 0.5 * shifted(CB[k + 1], cz, 1) if k < nb - 1 else zero
        before = jnp.where(low, swap_before, swap)
        after = jnp.where(low, swap, swap_after)
        diag = 6.0 * half + before + after
        CXM[k] = jnp.where(low, 0.0, half + before) if k == 0 else half + before
        CXP[k] = jnp.where(low, half + after, 0.0) if k == nb - 1 else half + after
        for ref, step, axis, edge in ((KYP, 1, 0, row == crows - 1), (KYM, -1, 0, row == 0),
                                      (KZP, 1, 1, z == cz - 1), (KZM, -1, 1, z == 0)):
            beside = jnp.where(edge, 0.0, shifted(half, step, axis))
            diag = diag + beside
            ref[k] = jnp.where(edge, 0.0, half + beside)
        DC[k] = diag
        IC[k] = 1.0 / diag

    XC[...] = jnp.zeros(XC.shape, jnp.float32)
    for copy in cr_first:
        copy.wait_recv()
    for copy in cr_second:
        copy.start()
    for copy in cr_second:
        copy.wait_recv()

    def total_of(value):
        return jnp.sum(jnp.sum(value, axis=0, keepdims=True), axis=1, keepdims=True)

    inner = pl.ds(HY, crows)
    acc = zero
    for k in range(nb):
        r = CR[k]
        zk = r * IC[k]
        RR[k] = r
        PP[k] = zk
        acc = acc + r * zk
    rz = total_of(acc)

    def iteration(step, rz):
        acc = zero
        images = []
        swaps = [shifted(PP[k], cz, 1) for k in range(nb)]
        for k in range(nb):
            p = PP[k]
            before = jnp.where(low, swaps[k - 1] if k > 0 else zero, swaps[k])
            after = jnp.where(low, swaps[k], swaps[k + 1] if k < nb - 1 else zero)
            total = CXM[k] * before + CXP[k] * after
            total += KYP[k] * shifted(p, 1, 0) + KYM[k] * shifted(p, -1, 0)
            total += KZP[k] * shifted(p, 1, 1) + KZM[k] * shifted(p, -1, 1)
            q = DC[k] * p - total
            images.append(q)
            acc = acc + p * q
        alpha = rz / total_of(acc)
        acc = zero
        preconds = []
        for k in range(nb):
            XC[k + 1, inner, :] += alpha * PP[k]
            r = RR[k] - alpha * images[k]
            RR[k] = r
            zk = r * IC[k]
            preconds.append(zk)
            acc = acc + r * zk
        new = total_of(acc)
        ratio = new / rz
        for k in range(nb):
            PP[k] = preconds[k] + ratio * PP[k]
        return new

    lax.fori_loop(0, ITERS, iteration, rz)

    wait_recv(pm_halo)
    window = pl.ds(pl.multiple_of(sub * cy, cy), cy + 2 * HY)
    for j in range(3):
        part = XC[box + j, window, :]
        wide = jnp.dot(part, spread, precision=HIGHEST, preferred_element_type=jnp.float32)
        for side in range(2):
            plane = wide[HY // 2:HY // 2 + mrows // 2, side * mz:(side + 1) * mz]
            TMP[pl.ds(0, mrows // 2, stride=2), :] = plane
            TMP[pl.ds(1, mrows // 2, stride=2), :] = plane
            copied = TMP[0:mrows, :]
            for twin in range(2):
                e = 4 * j + 2 * side + twin
                W[e] = PM[e] + copied
    medium_relax(0, 1, mx + 2 * HM - 1)
    medium_relax(1, 2, mx + 2 * HM - 2)

    for k in range(-2, mx + 2):
        plane = W[HM + k, pl.ds(HY // 2, rows // 2), :]
        TMP[pl.ds(0, rows // 2, stride=2), :] = plane
        TMP[pl.ds(1, rows // 2, stride=2), :] = plane
        wide = jnp.dot(TMP[0:rows, :], spread, precision=HIGHEST, preferred_element_type=jnp.float32)
        for e in (HB + 2 * k, HB + 2 * k + 1):
            V[e] = V[e] + wide
    fine_relax(0, HB - 2, HB + nx + 2)
    fine_relax(1, HB - 1, HB + nx + 1)

    @pl.loop(0, nx)
    def _(k):
        e = HB + k
        r_out[k] = fine_residual(e)
        p_out[k] = V[e, pl.ds(HY, ny), :]

    for copies in (beta_halo, rhs_halo, bm_halo, gm_halo, pm_halo):
        wait_send(copies)
    for copies in (cb_first, cb_second, cr_first, cr_second):
        for copy in copies:
            copy.wait_send()


def solution(mesh):
    nb, ns = mesh.shape["box"], mesh.shape["sub"]

    def shards(right_side, beta):
        nx, ny, nz = right_side.shape
        mx, my, mz = nx // 2, ny // 2, nz // 2
        fine = (nx + 2 * HB, ny + 2 * HY, nz)
        medium = (mx + 2 * HM, my + 2 * HY, mz)
        coarse = (nb, ns * (my // 2), mz)
        vmem = lambda shape, count: [pltpu.VMEM(shape, jnp.float32)] * count
        sems = pltpu.SemaphoreType.DMA
        return pl.pallas_call(
            functools.partial(kernel, nb, ns),
            out_shape=[jax.ShapeDtypeStruct((nx, ny, nz), jnp.float32)] * 2,
            in_specs=[pl.BlockSpec(memory_space=pl.ANY)] * 2,
            out_specs=[pl.BlockSpec(memory_space=pltpu.VMEM)] * 2,
            scratch_shapes=(
                vmem(fine, 10) + vmem((ny + 2 * HY, mz), 1) + vmem(medium, 11) + vmem(coarse, 2)
                + vmem((nb + 2, ns * (my // 2) + 2 * HY, mz), 1) + vmem(coarse, 8) + vmem(coarse, 2)
                + [sems((2,)), sems((2, 8)), sems((2, 8)), sems((3, 8)), sems((3, 8)),
                   sems((2, nb - 1)), sems((2, nb - 1)), sems((2, ns - 1)), sems((2, ns - 1))]),
            compiler_params=pltpu.CompilerParams(
                has_side_effects=True, vmem_limit_bytes=48 * 1024 * 1024),
        )(right_side, beta)

    placed = (P("box", "sub", None), P("box", "sub", None))
    return jax.shard_map(shards, mesh=mesh, in_specs=placed, out_specs=placed, check_vma=False)
```

```python
import functools

import jax
import jax.numpy as jnp
from jax import lax
from jax.experimental import pallas as pl
from jax.experimental.pallas import tpu as pltpu
from jax.sharding import PartitionSpec as P

ITERS = 8
HB = 3
HG = 2
HM = 4
HR = 3
HY = 8
DIRECTIONS = [(dx, dy) for dx in (-1, 0, 1) for dy in (-1, 0, 1) if (dx, dy) != (0, 0)]
HIGHEST = lax.Precision.HIGHEST


def span(step, size, width, halo):
    if step == 0:
        return 0, halo, size
    if step > 0:
        return size - width, halo - width, width
    return 0, halo + size, width


def shifted(value, step, axis):
    return pltpu.roll(value, (-step) % value.shape[axis], axis)


def kernel(nb, ns, g_in, b_in, p_out, r_out, B, G, CX, CYP, CYM, CZP, CZM, D, I, V, VP, TMP,
           BM, GM, MX, MYP, MYM, MZP, MZM, DM, IM, W, PM, CB, CR, XC, CXP, CXM, KYP, KYM, KZP, KZM, DC, IC,
           RR, PP, own_sem, fine_send, fine_recv, med_send, med_recv, all_send, all_recv):
    nx, ny, nz = g_in.shape
    mx, my, mz = nx // 2, ny // 2, nz // 2
    cy = my // 2
    rows, mrows = ny + 2 * HY, my + 2 * HY
    box, sub = lax.axis_index("box"), lax.axis_index("sub")

    def exists(dx, dy):
        ok = None
        for step, at, size in ((dx, box, nb), (dy, sub, ns)):
            here = None if step == 0 else (at + step < size if step > 0 else at + step >= 0)
            ok = here if ok is None else (ok if here is None else jnp.logical_and(ok, here))
        return ok

    def halo(src, dst, own, width, halo_x, sends, recvs, from_ext):
        out = []
        for k, (dx, dy) in enumerate(DIRECTIONS):
            deep = width - 1 if dx and dy else width
            sx, tx, lx = span(dx, own[0], deep, halo_x)
            sy, ty, ly = span(dy, own[1], HY, HY)
            if from_ext:
                sx, sy = sx + halo_x, sy + HY
            out.append(pltpu.make_async_remote_copy(
                src_ref=src.at[pl.ds(sx, lx), pl.ds(sy, ly), :],
                dst_ref=dst.at[pl.ds(tx, lx), pl.ds(ty, ly), :],
                send_sem=sends.at[k], recv_sem=recvs.at[k],
                device_id={"box": box + dx, "sub": sub + dy},
                device_id_type=pl.DeviceIdType.MESH))
        return out

    def start(copies):
        for (dx, dy), copy in zip(DIRECTIONS, copies):
            pl.when(exists(dx, dy))(copy.start)

    def wait_recv(copies):
        for (dx, dy), copy in zip(DIRECTIONS, copies):
            pl.when(exists(-dx, -dy))(copy.wait_recv)

    def wait_send(copies):
        for (dx, dy), copy in zip(DIRECTIONS, copies):
            pl.when(exists(dx, dy))(copy.wait_send)

    def clear(dst, own, width, halo_x):
        for dx, dy in DIRECTIONS:
            deep = width - 1 if dx and dy else width
            _, tx, lx = span(dx, own[0], deep, halo_x)
            _, ty, ly = span(dy, own[1], HY, HY)

            @pl.when(jnp.logical_not(exists(-dx, -dy)))
            def _():
                dst[pl.ds(tx, lx), pl.ds(ty, ly), :] = jnp.zeros((lx, ly, dst.shape[2]), jnp.float32)

    beta_halo = halo(b_in, B, (nx, ny), HB, HB, fine_send.at[0], fine_recv.at[0], False)
    rhs_halo = halo(g_in, G, (nx, ny), HG, HB, fine_send.at[1], fine_recv.at[1], False)
    own_b = pltpu.make_async_copy(b_in, B.at[pl.ds(HB, nx), pl.ds(HY, ny), :], own_sem.at[0])
    own_g = pltpu.make_async_copy(g_in, G.at[pl.ds(HB, nx), pl.ds(HY, ny), :], own_sem.at[1])
    own_b.start()
    own_g.start()

    count = nb * ns

    def peer(k):
        return {"box": lax.rem(box + k // ns, nb), "sub": lax.rem(sub + k % ns, ns)}

    barrier = pltpu.get_barrier_semaphore()

    for k in range(1, count):
        pl.semaphore_signal(barrier, inc=1, device_id=peer(k), device_id_type=pl.DeviceIdType.MESH)

    pair_sum = (lax.broadcasted_iota(jnp.int32, (nz, mz), 0) >> 1
                == lax.broadcasted_iota(jnp.int32, (nz, mz), 1)).astype(jnp.float32)
    spread = (lax.broadcasted_iota(jnp.int32, (mz, nz), 1) >> 1
              == lax.broadcasted_iota(jnp.int32, (mz, nz), 0)).astype(jnp.float32)

    def restrict(planes, factor):
        n = planes.shape[0]
        TMP[0:n, :] = jnp.dot(planes, pair_sum, precision=HIGHEST, preferred_element_type=jnp.float32)
        return (TMP[pl.ds(0, n // 2, stride=2), :] + TMP[pl.ds(1, n // 2, stride=2), :]) * factor

    def pack(planes):
        return jnp.concatenate([planes[0] + planes[1], planes[2] + planes[3]], axis=1)

    own_rows = pl.ds(pl.multiple_of(sub * cy, cy), cy)

    def gather(buffer, index):
        def copy(k):
            block = buffer.at[pl.ds(box, 1), own_rows, :]
            return pltpu.make_async_remote_copy(
                src_ref=block, dst_ref=block, send_sem=all_send.at[index, k - 1], recv_sem=all_recv.at[index, k - 1],
                device_id=peer(k), device_id_type=pl.DeviceIdType.MESH)

        def over(action):
            for k in range(1, count):
                action(copy(k))
        return over

    gather_b, gather_r = gather(CB, 0), gather(CR, 1)

    own_b.wait()
    for k in range(mx):
        summed = B[HB + 2 * k, pl.ds(HY, ny), :] + B[HB + 2 * k + 1, pl.ds(HY, ny), :]
        BM[HM + k, pl.ds(HY, my), :] = restrict(summed, 0.125)
    CB[box, own_rows, :] = restrict(pack([BM[HM + k, pl.ds(HY, my), :] for k in range(mx)]), 0.125)
    pl.semaphore_wait(barrier, count - 1)
    start(beta_halo)
    start(rhs_halo)
    bm_halo = halo(BM, BM, (mx, my), HM, HM, med_send.at[0], med_recv.at[0], True)
    start(bm_halo)
    clear(B, (nx, ny), HB, HB)
    clear(G, (nx, ny), HG, HB)
    clear(VP, (nx, ny), HB, HB)
    clear(BM, (mx, my), HM, HM)
    clear(GM, (mx, my), HR, HM)
    clear(PM, (mx, my), HM, HM)
    gather_b(lambda copy: copy.start())

    def parity(shape):
        return (lax.broadcasted_iota(jnp.int32, shape, 0) + lax.broadcasted_iota(jnp.int32, shape, 1)) & 1

    def setup_plane(e, b_ref, x_ref, yp, ym, zp, zm, d_ref, i_ref):
        b = b_ref[e]
        lane = lax.broadcasted_iota(jnp.int32, b.shape, 1)
        half = 0.5 * b
        up, down = shifted(half, 1, 0), shifted(half, -1, 0)
        right = jnp.where(lane == b.shape[1] - 1, 0.0, shifted(half, 1, 1))
        left = jnp.where(lane == 0, 0.0, shifted(half, -1, 1))
        before, after = 0.5 * b_ref[e - 1], 0.5 * b_ref[e + 1]
        x_ref[e] = half + after
        yp[e] = half + up
        ym[e] = half + down
        zp[e] = jnp.where(lane == b.shape[1] - 1, 0.0, half + right)
        zm[e] = jnp.where(lane == 0, 0.0, half + left)
        diag = 6.0 * half + ((before + after) + (up + down) + (right + left))
        inverse = jnp.where(b > 0.0, 1.0 / diag, 0.0)
        d_ref[e] = diag
        i_ref[e] = inverse
        return inverse

    def neighbours(e, v_ref, x_ref, yp, ym, zp, zm, cut=slice(None)):
        v = v_ref[e]
        total = x_ref[e] * v_ref[e + 1] + x_ref[e - 1] * v_ref[e - 1]
        total += yp[e] * shifted(v, 1, 0) + ym[e] * shifted(v, -1, 0)
        total += zp[e] * shifted(v, 1, 1) + zm[e] * shifted(v, -1, 1)
        return total, v

    fine = (CX, CYP, CYM, CZP, CZM)
    medium = (MX, MYP, MYM, MZP, MZM)
    fine_parity, medium_parity = parity((rows, nz)), parity((mrows, mz))

    def fine_relax(colour, low, high):
        @pl.loop(low, high)
        def _(e):
            total, v = neighbours(e, V, *fine)
            V[e] = jnp.where(fine_parity == ((e + HB + colour) & 1), (G[e] + total) * I[e], v)

    def medium_relax(colour, low, high):
        @pl.loop(low, high)
        def _(e):
            total, v = neighbours(e, W, *medium)
            W[e] = jnp.where(medium_parity == ((e + HM + colour) & 1), (GM[e] + total) * IM[e], v)

    own_g.wait()
    wait_recv(beta_halo)
    wait_recv(rhs_halo)

    CX[0] = 0.5 * (B[0] + B[1])

    @pl.loop(1, nx + 2 * HB - 1)
    def _(e):
        inverse = setup_plane(e, B, *fine, D, I)
        V[e] = jnp.where(fine_parity == ((e + HB) & 1), G[e] * inverse, 0.0)

    fine_relax(1, 2, nx + 2 * HB - 2)

    def fine_residual(e):
        total, v = neighbours(e, V, *fine)
        return (G[e] - (D[e] * v - total))[HY:HY + ny]

    @pl.loop(0, mx)
    def _(k):
        summed = fine_residual(HB + 2 * k) + fine_residual(HB + 2 * k + 1)
        VP[HB + 2 * k, pl.ds(HY, ny), :] = V[HB + 2 * k, pl.ds(HY, ny), :]
        VP[HB + 2 * k + 1, pl.ds(HY, ny), :] = V[HB + 2 * k + 1, pl.ds(HY, ny), :]
        GM[HM + k, pl.ds(HY, my), :] = restrict(summed, 0.5)

    gm_halo = halo(GM, GM, (mx, my), HR, HM, med_send.at[1], med_recv.at[1], True)
    start(gm_halo)
    pre_halo = halo(VP, VP, (nx, ny), HB, HB, fine_send.at[2], fine_recv.at[2], True)
    start(pre_halo)

    wait_recv(bm_halo)
    MX[0] = 0.5 * (BM[0] + BM[1])

    @pl.loop(1, mx + 2 * HM - 1)
    def _(e):
        setup_plane(e, BM, *medium, DM, IM)

    wait_recv(gm_halo)

    @pl.loop(HM - 2, HM + mx + 2)
    def _(e):
        W[e] = jnp.where(medium_parity == ((e + HM) & 1), GM[e] * IM[e], 0.0)

    medium_relax(1, HM - 1, HM + mx + 1)
    residuals = []
    for k in range(mx):
        total, v = neighbours(HM + k, W, *medium)
        residuals.append((GM[HM + k] - (DM[HM + k] * v - total))[HY:HY + my])
        PM[HM + k, pl.ds(HY, my), :] = v[HY:HY + my]
    CR[box, own_rows, :] = restrict(pack(residuals), 0.5)
    gather_r(lambda copy: copy.start())
    pm_halo = halo(PM, PM, (mx, my), HM, HM, med_send.at[2], med_recv.at[2], True)
    start(pm_halo)

    gather_b(lambda copy: copy.wait_recv())
    crows = ns * cy
    cz = mz // 2
    lane = lax.broadcasted_iota(jnp.int32, (crows, mz), 1)
    row = lax.broadcasted_iota(jnp.int32, (crows, mz), 0)
    low = lane < cz
    z = lane & (cz - 1)
    zero = jnp.zeros((crows, mz), jnp.float32)
    for k in range(nb):
        half = 0.5 * CB[k]
        swap = shifted(half, cz, 1)
        swap_before = 0.5 * shifted(CB[k - 1], cz, 1) if k > 0 else zero
        swap_after = 0.5 * shifted(CB[k + 1], cz, 1) if k < nb - 1 else zero
        before = jnp.where(low, swap_before, swap)
        after = jnp.where(low, swap, swap_after)
        diag = 6.0 * half + before + after
        CXM[k] = jnp.where(low, 0.0, half + before) if k == 0 else half + before
        CXP[k] = jnp.where(low, half + after, 0.0) if k == nb - 1 else half + after
        for ref, step, axis, edge in ((KYP, 1, 0, row == crows - 1), (KYM, -1, 0, row == 0),
                                      (KZP, 1, 1, z == cz - 1), (KZM, -1, 1, z == 0)):
            beside = jnp.where(edge, 0.0, shifted(half, step, axis))
            diag = diag + beside
            ref[k] = jnp.where(edge, 0.0, half + beside)
        DC[k] = diag
        IC[k] = 1.0 / diag

    XC[...] = jnp.zeros(XC.shape, jnp.float32)
    gather_r(lambda copy: copy.wait_recv())

    def total_of(value):
        return jnp.sum(jnp.sum(value, axis=0, keepdims=True), axis=1, keepdims=True)

    inner = pl.ds(HY, crows)
    acc = zero
    for k in range(nb):
        r = CR[k]
        zk = r * IC[k]
        RR[k] = r
        PP[k] = zk
        acc = acc + r * zk
    rz = total_of(acc)

    def iteration(step, rz):
        acc = zero
        images = []
        swaps = [shifted(PP[k], cz, 1) for k in range(nb)]
        for k in range(nb):
            p = PP[k]
            before = jnp.where(low, swaps[k - 1] if k > 0 else zero, swaps[k])
            after = jnp.where(low, swaps[k], swaps[k + 1] if k < nb - 1 else zero)
            total = CXM[k] * before + CXP[k] * after
            total += KYP[k] * shifted(p, 1, 0) + KYM[k] * shifted(p, -1, 0)
            total += KZP[k] * shifted(p, 1, 1) + KZM[k] * shifted(p, -1, 1)
            q = DC[k] * p - total
            images.append(q)
            acc = acc + p * q
        alpha = rz / total_of(acc)
        acc = zero
        preconds = []
        for k in range(nb):
            XC[k + 1, inner, :] += alpha * PP[k]
            r = RR[k] - alpha * images[k]
            RR[k] = r
            zk = r * IC[k]
            preconds.append(zk)
            acc = acc + r * zk
        new = total_of(acc)
        ratio = new / rz
        for k in range(nb):
            PP[k] = preconds[k] + ratio * PP[k]
        return new

    lax.fori_loop(0, ITERS, iteration, rz)

    wait_recv(pm_halo)
    window = pl.ds(pl.multiple_of(sub * cy, cy), cy + 2 * HY)
    for j in range(3):
        part = XC[box + j, window, :]
        wide = jnp.dot(part, spread, precision=HIGHEST, preferred_element_type=jnp.float32)
        for side in range(2):
            plane = wide[HY // 2:HY // 2 + mrows // 2, side * mz:(side + 1) * mz]
            TMP[pl.ds(0, mrows // 2, stride=2), :] = plane
            TMP[pl.ds(1, mrows // 2, stride=2), :] = plane
            copied = TMP[0:mrows, :]
            for twin in range(2):
                e = 4 * j + 2 * side + twin
                W[e] = PM[e] + copied
    medium_relax(0, 1, mx + 2 * HM - 1)
    medium_relax(1, 2, mx + 2 * HM - 2)

    wait_recv(pre_halo)
    for k in range(-2, mx + 2):
        plane = W[HM + k, pl.ds(HY // 2, rows // 2), :]
        TMP[pl.ds(0, rows // 2, stride=2), :] = plane
        TMP[pl.ds(1, rows // 2, stride=2), :] = plane
        wide = jnp.dot(TMP[0:rows, :], spread, precision=HIGHEST, preferred_element_type=jnp.float32)
        for e in (HB + 2 * k, HB + 2 * k + 1):
            if 0 <= e < nx + 2 * HB:
                V[e] = VP[e] + wide
    fine_relax(0, HB - 2, HB + nx + 2)
    fine_relax(1, HB - 1, HB + nx + 1)

    @pl.loop(0, nx)
    def _(k):
        e = HB + k
        r_out[k] = fine_residual(e)
        p_out[k] = V[e, pl.ds(HY, ny), :]

    for copies in (beta_halo, rhs_halo, bm_halo, gm_halo, pm_halo, pre_halo):
        wait_send(copies)
    gather_b(lambda copy: copy.wait_send())
    gather_r(lambda copy: copy.wait_send())


def solution(mesh):
    nb, ns = mesh.shape["box"], mesh.shape["sub"]

    def shards(right_side, beta):
        nx, ny, nz = right_side.shape
        mx, my, mz = nx // 2, ny // 2, nz // 2
        fine = (nx + 2 * HB, ny + 2 * HY, nz)
        medium = (mx + 2 * HM, my + 2 * HY, mz)
        coarse = (nb, ns * (my // 2), mz)
        vmem = lambda shape, count: [pltpu.VMEM(shape, jnp.float32)] * count
        sems = pltpu.SemaphoreType.DMA
        return pl.pallas_call(
            functools.partial(kernel, nb, ns),
            out_shape=[jax.ShapeDtypeStruct((nx, ny, nz), jnp.float32)] * 2,
            in_specs=[pl.BlockSpec(memory_space=pltpu.HBM)] * 2,
            out_specs=[pl.BlockSpec(memory_space=pltpu.VMEM)] * 2,
            scratch_shapes=(
                vmem(fine, 11) + vmem((ny + 2 * HY, mz), 1) + vmem(medium, 11) + vmem(coarse, 2)
                + vmem((nb + 2, ns * (my // 2) + 2 * HY, mz), 1) + vmem(coarse, 8) + vmem(coarse, 2)
                + [sems((2,)), sems((3, 8)), sems((3, 8)), sems((3, 8)), sems((3, 8)),
                   sems((2, nb * ns - 1)), sems((2, nb * ns - 1))]),
            compiler_params=pltpu.CompilerParams(
                collective_id=0, has_side_effects=True, vmem_limit_bytes=48 * 1024 * 1024),
        )(right_side, beta)

    placed = (P("box", "sub", None), P("box", "sub", None))
    return jax.shard_map(shards, mesh=mesh, in_specs=placed, out_specs=placed, check_vma=False)
```

```python
import functools

import jax
import jax.numpy as jnp
from jax import lax
from jax.experimental import pallas as pl
from jax.experimental.pallas import tpu as pltpu
from jax.sharding import PartitionSpec as P

ITERS = 8
HB = 3
HG = 2
HM = 4
HR = 3
HY = 8
DIRECTIONS = [(dx, dy) for dx in (-1, 0, 1) for dy in (-1, 0, 1) if (dx, dy) != (0, 0)]
HIGHEST = lax.Precision.HIGHEST


def span(step, size, width, halo):
    if step == 0:
        return 0, halo, size
    if step > 0:
        return size - width, halo - width, width
    return 0, halo + size, width


def shifted(value, step, axis):
    return pltpu.roll(value, (-step) % value.shape[axis], axis)


def kernel(nb, ns, g_in, b_in, p_out, r_out, B, G, CX, CYP, CYM, CZP, CZM, D, I, V, VP, PS, PR, TMP,
           BM, GM, MX, MYP, MYM, MZP, MZM, DM, IM, W, PM, CB, CR, XC, CXP, CXM, KYP, KYM, KZP, KZM, DC, IC,
           RR, PP, own_sem, fine_send, fine_recv, med_send, med_recv, all_send, all_recv):
    nx, ny, nz = g_in.shape
    mx, my, mz = nx // 2, ny // 2, nz // 2
    cy = my // 2
    rows, mrows = ny + 2 * HY, my + 2 * HY
    box, sub = lax.axis_index("box"), lax.axis_index("sub")

    def exists(dx, dy):
        ok = None
        for step, at, size in ((dx, box, nb), (dy, sub, ns)):
            here = None if step == 0 else (at + step < size if step > 0 else at + step >= 0)
            ok = here if ok is None else (ok if here is None else jnp.logical_and(ok, here))
        return ok

    def halo(src, dst, own, width, halo_x, sends, recvs, from_ext, flat=False):
        out = []
        for k, (dx, dy) in enumerate(DIRECTIONS):
            if flat and dy:
                out.append(None)
                continue
            deep = width - 1 if dx and dy else width
            sx, tx, lx = span(dx, own[0], deep, halo_x)
            sy, ty, ly = span(dy, own[1], HY, HY)
            if from_ext:
                sx, sy = sx + halo_x, sy + HY
            out.append(pltpu.make_async_remote_copy(
                src_ref=src.at[pl.ds(sx, lx), pl.ds(sy, ly), :],
                dst_ref=dst.at[pl.ds(tx, lx), pl.ds(ty, ly), :],
                send_sem=sends.at[k], recv_sem=recvs.at[k],
                device_id={"box": box + dx, "sub": sub + dy},
                device_id_type=pl.DeviceIdType.MESH))
        return out

    def start(copies):
        for (dx, dy), copy in zip(DIRECTIONS, copies):
            if copy is not None:
                pl.when(exists(dx, dy))(copy.start)

    def wait_recv(copies):
        for (dx, dy), copy in zip(DIRECTIONS, copies):
            if copy is not None:
                pl.when(exists(-dx, -dy))(copy.wait_recv)

    def wait_send(copies):
        for (dx, dy), copy in zip(DIRECTIONS, copies):
            if copy is not None:
                pl.when(exists(dx, dy))(copy.wait_send)

    def packed_halo(sends, recvs):
        out = []
        for k, (dx, dy) in enumerate(DIRECTIONS):
            if dy == 0:
                out.append(None)
                continue
            sx, tx, lx = span(dx, nx, HB - 1, HB)
            at = 0 if dy > 0 else 1
            out.append(pltpu.make_async_remote_copy(
                src_ref=PS.at[at, pl.ds(sx, lx), :, :], dst_ref=PR.at[at, pl.ds(tx, lx), :, :],
                send_sem=sends.at[k], recv_sem=recvs.at[k],
                device_id={"box": box + dx, "sub": sub + dy},
                device_id_type=pl.DeviceIdType.MESH))

            @pl.when(jnp.logical_not(exists(-dx, -dy)))
            def _():
                PR[at, pl.ds(tx, lx), :, :] = jnp.zeros((lx, HY, nz), jnp.float32)
        return out

    def clear(dst, own, width, halo_x, flat=False):
        for dx, dy in DIRECTIONS:
            if flat and dy:
                continue
            deep = width - 1 if dx and dy else width
            _, tx, lx = span(dx, own[0], deep, halo_x)
            _, ty, ly = span(dy, own[1], HY, HY)

            @pl.when(jnp.logical_not(exists(-dx, -dy)))
            def _():
                dst[pl.ds(tx, lx), pl.ds(ty, ly), :] = jnp.zeros((lx, ly, dst.shape[2]), jnp.float32)

    beta_halo = halo(b_in, B, (nx, ny), HB, HB, fine_send.at[0], fine_recv.at[0], False, True)
    rhs_halo = halo(g_in, G, (nx, ny), HG, HB, fine_send.at[1], fine_recv.at[1], False, True)
    own_b = pltpu.make_async_copy(b_in, B.at[pl.ds(HB, nx), pl.ds(HY, ny), :], own_sem.at[0])
    own_g = pltpu.make_async_copy(g_in, G.at[pl.ds(HB, nx), pl.ds(HY, ny), :], own_sem.at[1])
    own_b.start()
    own_g.start()

    count = nb * ns

    def peer(k):
        return {"box": lax.rem(box + k // ns, nb), "sub": lax.rem(sub + k % ns, ns)}

    barrier = pltpu.get_barrier_semaphore()

    for k in range(1, count):
        pl.semaphore_signal(barrier, inc=1, device_id=peer(k), device_id_type=pl.DeviceIdType.MESH)

    pair_sum = (lax.broadcasted_iota(jnp.int32, (nz, mz), 0) >> 1
                == lax.broadcasted_iota(jnp.int32, (nz, mz), 1)).astype(jnp.float32)
    spread = (lax.broadcasted_iota(jnp.int32, (mz, nz), 1) >> 1
              == lax.broadcasted_iota(jnp.int32, (mz, nz), 0)).astype(jnp.float32)

    def restrict(planes, factor):
        n = planes.shape[0]
        TMP[0:n, :] = jnp.dot(planes, pair_sum, precision=HIGHEST, preferred_element_type=jnp.float32)
        return (TMP[pl.ds(0, n // 2, stride=2), :] + TMP[pl.ds(1, n // 2, stride=2), :]) * factor

    def pack(planes):
        return jnp.concatenate([planes[0] + planes[1], planes[2] + planes[3]], axis=1)

    own_rows = pl.ds(pl.multiple_of(sub * cy, cy), cy)

    def gather(buffer, index):
        def copy(k):
            block = buffer.at[pl.ds(box, 1), own_rows, :]
            return pltpu.make_async_remote_copy(
                src_ref=block, dst_ref=block, send_sem=all_send.at[index, k - 1], recv_sem=all_recv.at[index, k - 1],
                device_id=peer(k), device_id_type=pl.DeviceIdType.MESH)

        def over(action):
            for k in range(1, count):
                action(copy(k))
        return over

    gather_b, gather_r = gather(CB, 0), gather(CR, 1)

    own_b.wait()
    for k in range(mx):
        summed = B[HB + 2 * k, pl.ds(HY, ny), :] + B[HB + 2 * k + 1, pl.ds(HY, ny), :]
        BM[HM + k, pl.ds(HY, my), :] = restrict(summed, 0.125)
    CB[box, own_rows, :] = restrict(pack([BM[HM + k, pl.ds(HY, my), :] for k in range(mx)]), 0.125)
    own_g.wait()
    tile_row = lax.broadcasted_iota(jnp.int32, (HY, nz), 0)
    for e in range(nx):
        for at, edge, mine in ((0, ny, tile_row >= HY - HB), (1, HY, tile_row < HB)):
            rhs = pltpu.roll(G[HB + e, pl.ds(edge, HY), :], HY // 2, 0)
            PS[at, e] = jnp.where(mine, B[HB + e, pl.ds(edge, HY), :], rhs)
    pack_halo = packed_halo(fine_send.at[3], fine_recv.at[3])
    pl.semaphore_wait(barrier, count - 1)
    start(pack_halo)
    start(beta_halo)
    start(rhs_halo)
    bm_halo = halo(BM, BM, (mx, my), HM, HM, med_send.at[0], med_recv.at[0], True)
    start(bm_halo)
    clear(B, (nx, ny), HB, HB, True)
    clear(G, (nx, ny), HG, HB, True)
    clear(VP, (nx, ny), HB, HB)
    clear(BM, (mx, my), HM, HM)
    clear(GM, (mx, my), HR, HM)
    clear(PM, (mx, my), HM, HM)
    gather_b(lambda copy: copy.start())

    def parity(shape):
        return (lax.broadcasted_iota(jnp.int32, shape, 0) + lax.broadcasted_iota(jnp.int32, shape, 1)) & 1

    def setup_plane(e, b_ref, x_ref, yp, ym, zp, zm, d_ref, i_ref):
        b = b_ref[e]
        lane = lax.broadcasted_iota(jnp.int32, b.shape, 1)
        half = 0.5 * b
        up, down = shifted(half, 1, 0), shifted(half, -1, 0)
        right = jnp.where(lane == b.shape[1] - 1, 0.0, shifted(half, 1, 1))
        left = jnp.where(lane == 0, 0.0, shifted(half, -1, 1))
        before, after = 0.5 * b_ref[e - 1], 0.5 * b_ref[e + 1]
        x_ref[e] = half + after
        yp[e] = half + up
        ym[e] = half + down
        zp[e] = jnp.where(lane == b.shape[1] - 1, 0.0, half + right)
        zm[e] = jnp.where(lane == 0, 0.0, half + left)
        diag = 6.0 * half + ((before + after) + (up + down) + (right + left))
        inverse = jnp.where(b > 0.0, 1.0 / diag, 0.0)
        d_ref[e] = diag
        i_ref[e] = inverse
        return inverse

    def neighbours(e, v_ref, x_ref, yp, ym, zp, zm, cut=slice(None)):
        v = v_ref[e]
        total = x_ref[e] * v_ref[e + 1] + x_ref[e - 1] * v_ref[e - 1]
        total += yp[e] * shifted(v, 1, 0) + ym[e] * shifted(v, -1, 0)
        total += zp[e] * shifted(v, 1, 1) + zm[e] * shifted(v, -1, 1)
        return total, v

    fine = (CX, CYP, CYM, CZP, CZM)
    medium = (MX, MYP, MYM, MZP, MZM)
    fine_parity, medium_parity = parity((rows, nz)), parity((mrows, mz))

    def fine_relax(colour, low, high):
        @pl.loop(low, high)
        def _(e):
            total, v = neighbours(e, V, *fine)
            V[e] = jnp.where(fine_parity == ((e + HB + colour) & 1), (G[e] + total) * I[e], v)

    def medium_relax(colour, low, high):
        @pl.loop(low, high)
        def _(e):
            total, v = neighbours(e, W, *medium)
            W[e] = jnp.where(medium_parity == ((e + HM + colour) & 1), (GM[e] + total) * IM[e], v)

    wait_recv(beta_halo)
    wait_recv(rhs_halo)
    wait_recv(pack_halo)
    for e in range(1, nx + 2 * HB - 1):
        for at, edge in ((0, 0), (1, HY + ny)):
            both = PR[at, e]
            B[e, pl.ds(edge, HY), :] = both
            G[e, pl.ds(edge, HY), :] = pltpu.roll(both, HY // 2, 0)

    CX[0] = 0.5 * (B[0] + B[1])

    @pl.loop(1, nx + 2 * HB - 1)
    def _(e):
        inverse = setup_plane(e, B, *fine, D, I)
        V[e] = jnp.where(fine_parity == ((e + HB) & 1), G[e] * inverse, 0.0)

    fine_relax(1, 2, nx + 2 * HB - 2)

    def fine_residual(e):
        total, v = neighbours(e, V, *fine)
        return (G[e] - (D[e] * v - total))[HY:HY + ny]

    @pl.loop(0, mx)
    def _(k):
        summed = fine_residual(HB + 2 * k) + fine_residual(HB + 2 * k + 1)
        VP[HB + 2 * k, pl.ds(HY, ny), :] = V[HB + 2 * k, pl.ds(HY, ny), :]
        VP[HB + 2 * k + 1, pl.ds(HY, ny), :] = V[HB + 2 * k + 1, pl.ds(HY, ny), :]
        GM[HM + k, pl.ds(HY, my), :] = restrict(summed, 0.5)

    gm_halo = halo(GM, GM, (mx, my), HR, HM, med_send.at[1], med_recv.at[1], True)
    start(gm_halo)
    pre_halo = halo(VP, VP, (nx, ny), HB, HB, fine_send.at[2], fine_recv.at[2], True)
    start(pre_halo)

    wait_recv(bm_halo)
    MX[0] = 0.5 * (BM[0] + BM[1])

    @pl.loop(1, mx + 2 * HM - 1)
    def _(e):
        setup_plane(e, BM, *medium, DM, IM)

    wait_recv(gm_halo)

    @pl.loop(HM - 2, HM + mx + 2)
    def _(e):
        W[e] = jnp.where(medium_parity == ((e + HM) & 1), GM[e] * IM[e], 0.0)

    medium_relax(1, HM - 1, HM + mx + 1)
    residuals = []
    for k in range(mx):
        total, v = neighbours(HM + k, W, *medium)
        residuals.append((GM[HM + k] - (DM[HM + k] * v - total))[HY:HY + my])
        PM[HM + k, pl.ds(HY, my), :] = v[HY:HY + my]
    CR[box, own_rows, :] = restrict(pack(residuals), 0.5)
    gather_r(lambda copy: copy.start())
    pm_halo = halo(PM, PM, (mx, my), HM, HM, med_send.at[2], med_recv.at[2], True)
    start(pm_halo)

    gather_b(lambda copy: copy.wait_recv())
    crows = ns * cy
    cz = mz // 2
    lane = lax.broadcasted_iota(jnp.int32, (crows, mz), 1)
    row = lax.broadcasted_iota(jnp.int32, (crows, mz), 0)
    low = lane < cz
    z = lane & (cz - 1)
    zero = jnp.zeros((crows, mz), jnp.float32)
    for k in range(nb):
        half = 0.5 * CB[k]
        swap = shifted(half, cz, 1)
        swap_before = 0.5 * shifted(CB[k - 1], cz, 1) if k > 0 else zero
        swap_after = 0.5 * shifted(CB[k + 1], cz, 1) if k < nb - 1 else zero
        before = jnp.where(low, swap_before, swap)
        after = jnp.where(low, swap, swap_after)
        diag = 6.0 * half + before + after
        CXM[k] = jnp.where(low, 0.0, half + before) if k == 0 else half + before
        CXP[k] = jnp.where(low, half + after, 0.0) if k == nb - 1 else half + after
        for ref, step, axis, edge in ((KYP, 1, 0, row == crows - 1), (KYM, -1, 0, row == 0),
                                      (KZP, 1, 1, z == cz - 1), (KZM, -1, 1, z == 0)):
            beside = jnp.where(edge, 0.0, shifted(half, step, axis))
            diag = diag + beside
            ref[k] = jnp.where(edge, 0.0, half + beside)
        DC[k] = diag
        IC[k] = 1.0 / diag

    XC[...] = jnp.zeros(XC.shape, jnp.float32)
    gather_r(lambda copy: copy.wait_recv())

    def total_of(value):
        return jnp.sum(jnp.sum(value, axis=0, keepdims=True), axis=1, keepdims=True)

    inner = pl.ds(HY, crows)
    acc = zero
    for k in range(nb):
        r = CR[k]
        zk = r * IC[k]
        RR[k] = r
        PP[k] = zk
        acc = acc + r * zk
    rz = total_of(acc)

    def iteration(step, rz):
        acc = zero
        images = []
        swaps = [shifted(PP[k], cz, 1) for k in range(nb)]
        for k in range(nb):
            p = PP[k]
            before = jnp.where(low, swaps[k - 1] if k > 0 else zero, swaps[k])
            after = jnp.where(low, swaps[k], swaps[k + 1] if k < nb - 1 else zero)
            total = CXM[k] * before + CXP[k] * after
            total += KYP[k] * shifted(p, 1, 0) + KYM[k] * shifted(p, -1, 0)
            total += KZP[k] * shifted(p, 1, 1) + KZM[k] * shifted(p, -1, 1)
            q = DC[k] * p - total
            images.append(q)
            acc = acc + p * q
        alpha = rz / total_of(acc)
        acc = zero
        preconds = []
        for k in range(nb):
            XC[k + 1, inner, :] += alpha * PP[k]
            r = RR[k] - alpha * images[k]
            RR[k] = r
            zk = r * IC[k]
            preconds.append(zk)
            acc = acc + r * zk
        new = total_of(acc)
        ratio = new / rz
        for k in range(nb):
            PP[k] = preconds[k] + ratio * PP[k]
        return new

    lax.fori_loop(0, ITERS, iteration, rz)

    wait_recv(pm_halo)
    window = pl.ds(pl.multiple_of(sub * cy, cy), cy + 2 * HY)
    for j in range(3):
        part = XC[box + j, window, :]
        wide = jnp.dot(part, spread, precision=HIGHEST, preferred_element_type=jnp.float32)
        for side in range(2):
            plane = wide[HY // 2:HY // 2 + mrows // 2, side * mz:(side + 1) * mz]
            TMP[pl.ds(0, mrows // 2, stride=2), :] = plane
            TMP[pl.ds(1, mrows // 2, stride=2), :] = plane
            copied = TMP[0:mrows, :]
            for twin in range(2):
                e = 4 * j + 2 * side + twin
                W[e] = PM[e] + copied
    medium_relax(0, 1, mx + 2 * HM - 1)
    medium_relax(1, 2, mx + 2 * HM - 2)

    wait_recv(pre_halo)
    for k in range(-2, mx + 2):
        plane = W[HM + k, pl.ds(HY // 2, rows // 2), :]
        TMP[pl.ds(0, rows // 2, stride=2), :] = plane
        TMP[pl.ds(1, rows // 2, stride=2), :] = plane
        wide = jnp.dot(TMP[0:rows, :], spread, precision=HIGHEST, preferred_element_type=jnp.float32)
        for e in (HB + 2 * k, HB + 2 * k + 1):
            if 0 <= e < nx + 2 * HB:
                V[e] = VP[e] + wide
    fine_relax(0, HB - 2, HB + nx + 2)
    fine_relax(1, HB - 1, HB + nx + 1)

    @pl.loop(0, nx)
    def _(k):
        e = HB + k
        r_out[k] = fine_residual(e)
        p_out[k] = V[e, pl.ds(HY, ny), :]

    for copies in (beta_halo, rhs_halo, bm_halo, gm_halo, pm_halo, pre_halo, pack_halo):
        wait_send(copies)
    gather_b(lambda copy: copy.wait_send())
    gather_r(lambda copy: copy.wait_send())


def solution(mesh):
    nb, ns = mesh.shape["box"], mesh.shape["sub"]

    def shards(right_side, beta):
        nx, ny, nz = right_side.shape
        mx, my, mz = nx // 2, ny // 2, nz // 2
        fine = (nx + 2 * HB, ny + 2 * HY, nz)
        medium = (mx + 2 * HM, my + 2 * HY, mz)
        coarse = (nb, ns * (my // 2), mz)
        vmem = lambda shape, count: [pltpu.VMEM(shape, jnp.float32)] * count
        sems = pltpu.SemaphoreType.DMA
        return pl.pallas_call(
            functools.partial(kernel, nb, ns),
            out_shape=[jax.ShapeDtypeStruct((nx, ny, nz), jnp.float32)] * 2,
            in_specs=[pl.BlockSpec(memory_space=pltpu.HBM)] * 2,
            out_specs=[pl.BlockSpec(memory_space=pltpu.VMEM)] * 2,
            scratch_shapes=(
                vmem(fine, 11) + vmem((2, nx, HY, nz), 1) + vmem((2, nx + 2 * HB, HY, nz), 1) + vmem((ny + 2 * HY, mz), 1) + vmem(medium, 11) + vmem(coarse, 2)
                + vmem((nb + 2, ns * (my // 2) + 2 * HY, mz), 1) + vmem(coarse, 8) + vmem(coarse, 2)
                + [sems((2,)), sems((4, 8)), sems((4, 8)), sems((3, 8)), sems((3, 8)),
                   sems((2, nb * ns - 1)), sems((2, nb * ns - 1))]),
            compiler_params=pltpu.CompilerParams(
                collective_id=0, has_side_effects=True, vmem_limit_bytes=48 * 1024 * 1024),
        )(right_side, beta)

    placed = (P("box", "sub", None), P("box", "sub", None))
    return jax.shard_map(shards, mesh=mesh, in_specs=placed, out_specs=placed, check_vma=False)
```

```python
import functools

import jax
import jax.numpy as jnp
from jax import lax
from jax.experimental import pallas as pl
from jax.experimental.pallas import tpu as pltpu
from jax.sharding import PartitionSpec as P

ITERS = 8
HB = 3
HG = 2
HM = 4
HR = 3
HY = 8
DIRECTIONS = [(dx, dy) for dx in (-1, 0, 1) for dy in (-1, 0, 1) if (dx, dy) != (0, 0)]
HIGHEST = lax.Precision.HIGHEST


def span(step, size, width, halo):
    if step == 0:
        return 0, halo, size
    if step > 0:
        return size - width, halo - width, width
    return 0, halo + size, width


def shifted(value, step, axis):
    return pltpu.roll(value, (-step) % value.shape[axis], axis)


def kernel(nb, ns, g_in, b_in, p_out, r_out, B, G, CX, CYP, CYM, CZP, CZM, D, I, V, VP, PS, PR, TMP,
           BM, GM, MX, MYP, MYM, MZP, MZM, DM, IM, W, PM, CB, CR, XC, CXP, CXM, KYP, KYM, KZP, KZM, DC, IC,
           RR, PP, own_sem, fine_send, fine_recv, med_send, med_recv, all_send, all_recv):
    nx, ny, nz = g_in.shape
    mx, my, mz = nx // 2, ny // 2, nz // 2
    cy = my // 2
    rows, mrows = ny + 2 * HY, my + 2 * HY
    box, sub = lax.axis_index("box"), lax.axis_index("sub")

    def exists(dx, dy):
        ok = None
        for step, at, size in ((dx, box, nb), (dy, sub, ns)):
            here = None if step == 0 else (at + step < size if step > 0 else at + step >= 0)
            ok = here if ok is None else (ok if here is None else jnp.logical_and(ok, here))
        return ok

    def halo(src, dst, own, width, halo_x, sends, recvs, from_ext, flat=False):
        out = []
        for k, (dx, dy) in enumerate(DIRECTIONS):
            if flat and dy:
                out.append(None)
                continue
            deep = width - 1 if dx and dy else width
            sx, tx, lx = span(dx, own[0], deep, halo_x)
            sy, ty, ly = span(dy, own[1], HY, HY)
            if from_ext:
                sx, sy = sx + halo_x, sy + HY
            out.append(pltpu.make_async_remote_copy(
                src_ref=src.at[pl.ds(sx, lx), pl.ds(sy, ly), :],
                dst_ref=dst.at[pl.ds(tx, lx), pl.ds(ty, ly), :],
                send_sem=sends.at[k], recv_sem=recvs.at[k],
                device_id={"box": box + dx, "sub": sub + dy},
                device_id_type=pl.DeviceIdType.MESH))
        return out

    def start(copies):
        for (dx, dy), copy in zip(DIRECTIONS, copies):
            if copy is not None:
                pl.when(exists(dx, dy))(copy.start)

    def wait_recv(copies):
        for (dx, dy), copy in zip(DIRECTIONS, copies):
            if copy is not None:
                pl.when(exists(-dx, -dy))(copy.wait_recv)

    def wait_send(copies):
        for (dx, dy), copy in zip(DIRECTIONS, copies):
            if copy is not None:
                pl.when(exists(dx, dy))(copy.wait_send)

    def packed_halo(sends, recvs):
        out = []
        for k, (dx, dy) in enumerate(DIRECTIONS):
            if dy == 0:
                out.append(None)
                continue
            sx, tx, lx = span(dx, nx, HB - 1, HB)
            at = 0 if dy > 0 else 1
            out.append(pltpu.make_async_remote_copy(
                src_ref=PS.at[at, pl.ds(sx, lx), :, :], dst_ref=PR.at[at, pl.ds(tx, lx), :, :],
                send_sem=sends.at[k], recv_sem=recvs.at[k],
                device_id={"box": box + dx, "sub": sub + dy},
                device_id_type=pl.DeviceIdType.MESH))

            @pl.when(jnp.logical_not(exists(-dx, -dy)))
            def _():
                PR[at, pl.ds(tx, lx), :, :] = jnp.zeros((lx, HY, nz), jnp.float32)
        return out

    def clear(dst, own, width, halo_x, flat=False):
        for dx, dy in DIRECTIONS:
            if flat and dy:
                continue
            deep = width - 1 if dx and dy else width
            _, tx, lx = span(dx, own[0], deep, halo_x)
            _, ty, ly = span(dy, own[1], HY, HY)

            @pl.when(jnp.logical_not(exists(-dx, -dy)))
            def _():
                dst[pl.ds(tx, lx), pl.ds(ty, ly), :] = jnp.zeros((lx, ly, dst.shape[2]), jnp.float32)

    beta_halo = halo(b_in, B, (nx, ny), HB, HB, fine_send.at[0], fine_recv.at[0], False, True)
    rhs_halo = halo(g_in, G, (nx, ny), HG, HB, fine_send.at[1], fine_recv.at[1], False, True)
    own_b = pltpu.make_async_copy(b_in, B.at[pl.ds(HB, nx), pl.ds(HY, ny), :], own_sem.at[0])
    own_g = pltpu.make_async_copy(g_in, G.at[pl.ds(HB, nx), pl.ds(HY, ny), :], own_sem.at[1])
    own_b.start()
    own_g.start()

    count = nb * ns

    def peer(k):
        return {"box": lax.rem(box + k // ns, nb), "sub": lax.rem(sub + k % ns, ns)}

    barrier = pltpu.get_barrier_semaphore()

    for k in range(1, count):
        pl.semaphore_signal(barrier, inc=1, device_id=peer(k), device_id_type=pl.DeviceIdType.MESH)

    pair_sum = (lax.broadcasted_iota(jnp.int32, (nz, mz), 0) >> 1
                == lax.broadcasted_iota(jnp.int32, (nz, mz), 1)).astype(jnp.float32)
    spread = (lax.broadcasted_iota(jnp.int32, (mz, nz), 1) >> 1
              == lax.broadcasted_iota(jnp.int32, (mz, nz), 0)).astype(jnp.float32)

    def restrict(planes, factor):
        n = planes.shape[0]
        TMP[0:n, :] = jnp.dot(planes, pair_sum, precision=HIGHEST, preferred_element_type=jnp.float32)
        return (TMP[pl.ds(0, n // 2, stride=2), :] + TMP[pl.ds(1, n // 2, stride=2), :]) * factor

    def pack(planes):
        return jnp.concatenate([planes[0] + planes[1], planes[2] + planes[3]], axis=1)

    own_rows = pl.ds(pl.multiple_of(sub * cy, cy), cy)

    def gather(buffer, index):
        def copy(k):
            block = buffer.at[pl.ds(box, 1), own_rows, :]
            return pltpu.make_async_remote_copy(
                src_ref=block, dst_ref=block, send_sem=all_send.at[index, k - 1], recv_sem=all_recv.at[index, k - 1],
                device_id=peer(k), device_id_type=pl.DeviceIdType.MESH)

        def over(action):
            for k in range(1, count):
                action(copy(k))
        return over

    gather_b, gather_r = gather(CB, 0), gather(CR, 1)

    own_b.wait()
    for k in range(mx):
        summed = B[HB + 2 * k, pl.ds(HY, ny), :] + B[HB + 2 * k + 1, pl.ds(HY, ny), :]
        BM[HM + k, pl.ds(HY, my), :] = restrict(summed, 0.125)
    CB[box, own_rows, :] = restrict(pack([BM[HM + k, pl.ds(HY, my), :] for k in range(mx)]), 0.125)
    own_g.wait()
    tile_row = lax.broadcasted_iota(jnp.int32, (HY, nz), 0)
    for e in range(nx):
        for at, edge, mine in ((0, ny, tile_row >= HY - HB), (1, HY, tile_row < HB)):
            rhs = pltpu.roll(G[HB + e, pl.ds(edge, HY), :], HY // 2, 0)
            PS[at, e] = jnp.where(mine, B[HB + e, pl.ds(edge, HY), :], rhs)
    pack_halo = packed_halo(fine_send.at[3], fine_recv.at[3])
    pl.semaphore_wait(barrier, count - 1)
    start(pack_halo)
    start(beta_halo)
    start(rhs_halo)
    bm_halo = halo(BM, BM, (mx, my), HM, HM, med_send.at[0], med_recv.at[0], True)
    start(bm_halo)
    clear(B, (nx, ny), HB, HB, True)
    clear(G, (nx, ny), HG, HB, True)
    clear(VP, (nx, ny), HB, HB)
    clear(BM, (mx, my), HM, HM)
    clear(GM, (mx, my), HR, HM)
    clear(PM, (mx, my), HM, HM)

    def parity(shape):
        return (lax.broadcasted_iota(jnp.int32, shape, 0) + lax.broadcasted_iota(jnp.int32, shape, 1)) & 1

    def setup_plane(e, b_ref, x_ref, yp, ym, zp, zm, d_ref, i_ref):
        b = b_ref[e]
        lane = lax.broadcasted_iota(jnp.int32, b.shape, 1)
        half = 0.5 * b
        up, down = shifted(half, 1, 0), shifted(half, -1, 0)
        right = jnp.where(lane == b.shape[1] - 1, 0.0, shifted(half, 1, 1))
        left = jnp.where(lane == 0, 0.0, shifted(half, -1, 1))
        before, after = 0.5 * b_ref[e - 1], 0.5 * b_ref[e + 1]
        x_ref[e] = half + after
        yp[e] = half + up
        ym[e] = half + down
        zp[e] = jnp.where(lane == b.shape[1] - 1, 0.0, half + right)
        zm[e] = jnp.where(lane == 0, 0.0, half + left)
        diag = 6.0 * half + ((before + after) + (up + down) + (right + left))
        inverse = jnp.where(b > 0.0, 1.0 / diag, 0.0)
        d_ref[e] = diag
        i_ref[e] = inverse
        return inverse

    def neighbours(e, v_ref, x_ref, yp, ym, zp, zm, cut=slice(None)):
        v = v_ref[e]
        total = x_ref[e] * v_ref[e + 1] + x_ref[e - 1] * v_ref[e - 1]
        total += yp[e] * shifted(v, 1, 0) + ym[e] * shifted(v, -1, 0)
        total += zp[e] * shifted(v, 1, 1) + zm[e] * shifted(v, -1, 1)
        return total, v

    fine = (CX, CYP, CYM, CZP, CZM)
    medium = (MX, MYP, MYM, MZP, MZM)
    fine_parity, medium_parity = parity((rows, nz)), parity((mrows, mz))

    def fine_relax(colour, low, high):
        @pl.loop(low, high)
        def _(e):
            total, v = neighbours(e, V, *fine)
            V[e] = jnp.where(fine_parity == ((e + HB + colour) & 1), (G[e] + total) * I[e], v)

    def medium_relax(colour, low, high):
        @pl.loop(low, high)
        def _(e):
            total, v = neighbours(e, W, *medium)
            W[e] = jnp.where(medium_parity == ((e + HM + colour) & 1), (GM[e] + total) * IM[e], v)

    wait_recv(beta_halo)
    wait_recv(rhs_halo)
    wait_recv(pack_halo)
    for e in range(1, nx + 2 * HB - 1):
        for at, edge in ((0, 0), (1, HY + ny)):
            both = PR[at, e]
            B[e, pl.ds(edge, HY), :] = both
            G[e, pl.ds(edge, HY), :] = pltpu.roll(both, HY // 2, 0)

    CX[0] = 0.5 * (B[0] + B[1])

    @pl.loop(1, nx + 2 * HB - 1)
    def _(e):
        inverse = setup_plane(e, B, *fine, D, I)
        V[e] = jnp.where(fine_parity == ((e + HB) & 1), G[e] * inverse, 0.0)

    fine_relax(1, 2, nx + 2 * HB - 2)

    def fine_residual(e):
        total, v = neighbours(e, V, *fine)
        return (G[e] - (D[e] * v - total))[HY:HY + ny]

    @pl.loop(0, mx)
    def _(k):
        summed = fine_residual(HB + 2 * k) + fine_residual(HB + 2 * k + 1)
        VP[HB + 2 * k, pl.ds(HY, ny), :] = V[HB + 2 * k, pl.ds(HY, ny), :]
        VP[HB + 2 * k + 1, pl.ds(HY, ny), :] = V[HB + 2 * k + 1, pl.ds(HY, ny), :]
        GM[HM + k, pl.ds(HY, my), :] = restrict(summed, 0.5)

    gm_halo = halo(GM, GM, (mx, my), HR, HM, med_send.at[1], med_recv.at[1], True)
    start(gm_halo)
    gather_b(lambda copy: copy.start())
    pre_halo = halo(VP, VP, (nx, ny), HB, HB, fine_send.at[2], fine_recv.at[2], True)

    wait_recv(bm_halo)
    MX[0] = 0.5 * (BM[0] + BM[1])

    @pl.loop(1, mx + 2 * HM - 1)
    def _(e):
        setup_plane(e, BM, *medium, DM, IM)

    wait_recv(gm_halo)

    @pl.loop(HM - 2, HM + mx + 2)
    def _(e):
        W[e] = jnp.where(medium_parity == ((e + HM) & 1), GM[e] * IM[e], 0.0)

    medium_relax(1, HM - 1, HM + mx + 1)
    residuals = []
    for k in range(mx):
        total, v = neighbours(HM + k, W, *medium)
        residuals.append((GM[HM + k] - (DM[HM + k] * v - total))[HY:HY + my])
        PM[HM + k, pl.ds(HY, my), :] = v[HY:HY + my]
    CR[box, own_rows, :] = restrict(pack(residuals), 0.5)
    gather_r(lambda copy: copy.start())
    pm_halo = halo(PM, PM, (mx, my), HM, HM, med_send.at[2], med_recv.at[2], True)
    start(pm_halo)
    start(pre_halo)

    gather_b(lambda copy: copy.wait_recv())
    crows = ns * cy
    cz = mz // 2
    lane = lax.broadcasted_iota(jnp.int32, (crows, mz), 1)
    row = lax.broadcasted_iota(jnp.int32, (crows, mz), 0)
    low = lane < cz
    z = lane & (cz - 1)
    zero = jnp.zeros((crows, mz), jnp.float32)
    for k in range(nb):
        half = 0.5 * CB[k]
        swap = shifted(half, cz, 1)
        swap_before = 0.5 * shifted(CB[k - 1], cz, 1) if k > 0 else zero
        swap_after = 0.5 * shifted(CB[k + 1], cz, 1) if k < nb - 1 else zero
        before = jnp.where(low, swap_before, swap)
        after = jnp.where(low, swap, swap_after)
        diag = 6.0 * half + before + after
        CXM[k] = jnp.where(low, 0.0, half + before) if k == 0 else half + before
        CXP[k] = jnp.where(low, half + after, 0.0) if k == nb - 1 else half + after
        for ref, step, axis, edge in ((KYP, 1, 0, row == crows - 1), (KYM, -1, 0, row == 0),
                                      (KZP, 1, 1, z == cz - 1), (KZM, -1, 1, z == 0)):
            beside = jnp.where(edge, 0.0, shifted(half, step, axis))
            diag = diag + beside
            ref[k] = jnp.where(edge, 0.0, half + beside)
        DC[k] = diag
        IC[k] = 1.0 / diag

    XC[...] = jnp.zeros(XC.shape, jnp.float32)
    gather_r(lambda copy: copy.wait_recv())

    def total_of(value):
        return jnp.sum(jnp.sum(value, axis=0, keepdims=True), axis=1, keepdims=True)

    inner = pl.ds(HY, crows)
    acc = zero
    for k in range(nb):
        r = CR[k]
        zk = r * IC[k]
        RR[k] = r
        PP[k] = zk
        acc = acc + r * zk
    rz = total_of(acc)

    def iteration(step, rz):
        acc = zero
        images = []
        swaps = [shifted(PP[k], cz, 1) for k in range(nb)]
        for k in range(nb):
            p = PP[k]
            before = jnp.where(low, swaps[k - 1] if k > 0 else zero, swaps[k])
            after = jnp.where(low, swaps[k], swaps[k + 1] if k < nb - 1 else zero)
            total = CXM[k] * before + CXP[k] * after
            total += KYP[k] * shifted(p, 1, 0) + KYM[k] * shifted(p, -1, 0)
            total += KZP[k] * shifted(p, 1, 1) + KZM[k] * shifted(p, -1, 1)
            q = DC[k] * p - total
            images.append(q)
            acc = acc + p * q
        alpha = rz / total_of(acc)
        acc = zero
        preconds = []
        for k in range(nb):
            XC[k + 1, inner, :] += alpha * PP[k]
            r = RR[k] - alpha * images[k]
            RR[k] = r
            zk = r * IC[k]
            preconds.append(zk)
            acc = acc + r * zk
        new = total_of(acc)
        ratio = new / rz
        for k in range(nb):
            PP[k] = preconds[k] + ratio * PP[k]
        return new

    lax.fori_loop(0, ITERS, iteration, rz)

    wait_recv(pm_halo)
    window = pl.ds(pl.multiple_of(sub * cy, cy), cy + 2 * HY)
    for j in range(3):
        part = XC[box + j, window, :]
        wide = jnp.dot(part, spread, precision=HIGHEST, preferred_element_type=jnp.float32)
        for side in range(2):
            plane = wide[HY // 2:HY // 2 + mrows // 2, side * mz:(side + 1) * mz]
            TMP[pl.ds(0, mrows // 2, stride=2), :] = plane
            TMP[pl.ds(1, mrows // 2, stride=2), :] = plane
            copied = TMP[0:mrows, :]
            for twin in range(2):
                e = 4 * j + 2 * side + twin
                W[e] = PM[e] + copied
    medium_relax(0, 1, mx + 2 * HM - 1)
    medium_relax(1, 2, mx + 2 * HM - 2)

    wait_recv(pre_halo)
    for k in range(-2, mx + 2):
        plane = W[HM + k, pl.ds(HY // 2, rows // 2), :]
        TMP[pl.ds(0, rows // 2, stride=2), :] = plane
        TMP[pl.ds(1, rows // 2, stride=2), :] = plane
        wide = jnp.dot(TMP[0:rows, :], spread, precision=HIGHEST, preferred_element_type=jnp.float32)
        for e in (HB + 2 * k, HB + 2 * k + 1):
            if 0 <= e < nx + 2 * HB:
                V[e] = VP[e] + wide
    fine_relax(0, HB - 2, HB + nx + 2)
    fine_relax(1, HB - 1, HB + nx + 1)

    @pl.loop(0, nx)
    def _(k):
        e = HB + k
        r_out[k] = fine_residual(e)
        p_out[k] = V[e, pl.ds(HY, ny), :]

    for copies in (beta_halo, rhs_halo, bm_halo, gm_halo, pm_halo, pre_halo, pack_halo):
        wait_send(copies)
    gather_b(lambda copy: copy.wait_send())
    gather_r(lambda copy: copy.wait_send())


def solution(mesh):
    nb, ns = mesh.shape["box"], mesh.shape["sub"]

    def shards(right_side, beta):
        nx, ny, nz = right_side.shape
        mx, my, mz = nx // 2, ny // 2, nz // 2
        fine = (nx + 2 * HB, ny + 2 * HY, nz)
        medium = (mx + 2 * HM, my + 2 * HY, mz)
        coarse = (nb, ns * (my // 2), mz)
        vmem = lambda shape, count: [pltpu.VMEM(shape, jnp.float32)] * count
        sems = pltpu.SemaphoreType.DMA
        return pl.pallas_call(
            functools.partial(kernel, nb, ns),
            out_shape=[jax.ShapeDtypeStruct((nx, ny, nz), jnp.float32)] * 2,
            in_specs=[pl.BlockSpec(memory_space=pltpu.HBM)] * 2,
            out_specs=[pl.BlockSpec(memory_space=pltpu.VMEM)] * 2,
            scratch_shapes=(
                vmem(fine, 11) + vmem((2, nx, HY, nz), 1) + vmem((2, nx + 2 * HB, HY, nz), 1) + vmem((ny + 2 * HY, mz), 1) + vmem(medium, 11) + vmem(coarse, 2)
                + vmem((nb + 2, ns * (my // 2) + 2 * HY, mz), 1) + vmem(coarse, 8) + vmem(coarse, 2)
                + [sems((2,)), sems((4, 8)), sems((4, 8)), sems((3, 8)), sems((3, 8)),
                   sems((2, nb * ns - 1)), sems((2, nb * ns - 1))]),
            compiler_params=pltpu.CompilerParams(
                collective_id=0, has_side_effects=True, vmem_limit_bytes=48 * 1024 * 1024),
        )(right_side, beta)

    placed = (P("box", "sub", None), P("box", "sub", None))
    return jax.shard_map(shards, mesh=mesh, in_specs=placed, out_specs=placed, check_vma=False)
```
